32 devices in a mesh: dom: 2 (over x), store: 8 (over z, y), mp: 2 (over core).
Axes of the slice: x: 2, y: 2, z: 4, core: 2. Of those that a mesh axis runs over, the one named last changes fastest.
Arguments:
- layer_input: bfloat16 [16, 512, 8192], P('dom', 'store', 'mp'), parts along dimension 0, may hold values from -6 to 6
- out_grad: bfloat16 [16, 512, 8192], P('dom', 'store', 'mp'), parts along dimension 0, may hold values from -6 to 6
- proj_in: bfloat16 [64, 8192], P(None, 'mp'), may hold values from -0.0625 to 0.0625
- proj_out: bfloat16 [64, 8192], P(None, 'mp'), may hold values from -0.0625 to 0.0625
- counts: int32 [16], P('dom'), parts along dimension 0, may hold values from 256 to 512, as said below
- store_rows: bfloat16 [12288, 4096], P(('dom', 'store', 'mp')), parts along dimension 0, may hold values from -6 to 6
- doc_ids: int32 [12288], P(('dom', 'store', 'mp')), parts along dimension 0, may hold values from 0 to 191, never falling along the last dimension, each value on 1 to 64 neighbouring positions
Outputs:
- query_grads: float32 [16, 4096], P('dom'), parts along dimension 0
- row_scores: float32 [16, 6144], P('dom', ('store', 'mp')), parts along dimension 0
- doc_scores: float32 [16, 6144], P('dom', ('store', 'mp')), parts along dimension 0
The draws below stay inside these ranges and needn't reach their ends.
There are 2 independent parts, one for each index of `dom`. The reference program is written for one: setup_inputs(seed, part) draws one part's arguments, and reference() takes and returns one part's arrays. A program takes and returns all parts, laid end to end along the dimension named above; an argument that names none is the same for every part. Nothing has to cross between parts.
Inputs may be any that keep to these rules, and one draw needn't show every extreme that they name: `counts`: some query example has exactly 512 real tokens and some exactly 256. `doc_ids`: each dom group numbers its own training examples from 0 to 191. Within one group the rows of one training example are consecutive, ids never fall along the rows, and one example has exactly 64 rows.
All inputs are finite; a program needn't handle non-finite values.
Results may differ from the reference program's by a relative error of at most 0.0029.
Values sent between devices are 32-bit elements; how exact they have to be, the bound alone decides.
A program may use at most 64 MiB of HBM per device.

```python
import math
import jax
import jax.numpy as jnp
import numpy as np
from jax import lax

D = 8192
KI = 64
KO = 64
QUERIES = 8
MOST = 64
LEN = 512
ROWS = 6144
DOCS = 192


def draw_counts(key, part):
    key = jax.random.fold_in(key, 7)
    lengths = jax.random.randint(key, (QUERIES,), LEN // 2, LEN + 1)
    chosen = jax.random.randint(jax.random.fold_in(key, 1), (), 0, QUERIES)
    places = jnp.arange(QUERIES)
    lengths = jnp.where(places == chosen, LEN, lengths)
    lengths = jnp.where(places == (chosen + 1) % QUERIES, LEN // 2, lengths)
    return lengths.astype(jnp.int32)


def shard_levels(rng, dims, shards, low, largest):
    level, own = 1.0, jax.random.fold_in(rng, 6)
    for axis_at, blocks in shards:
        steps = jnp.exp(jax.random.uniform(jax.random.fold_in(own, axis_at), (blocks,), jnp.float32, low / len(shards), largest / len(shards)))
        level = level * jnp.repeat(steps, dims[axis_at] // blocks).reshape([-1 if axis == axis_at else 1 for axis in range(len(dims))])
    return level


def profile(number_of, total, bound, lean):
    portions = [(1 << 20) // math.isqrt(grade ** lean) + 1 for grade in range(2, number_of + 1)]
    surplus, holding = total - bound - (number_of - 1), [1] * (number_of - 1)
    while surplus > 0:
        free = [i for i in range(number_of - 1) if holding[i] < bound]
        pool, remaining = sum([portions[i] for i in free]), surplus
        for i in free:
            addition = min(bound - holding[i], max(1, remaining * portions[i] // pool), surplus)
            holding[i] = holding[i] + addition
            surplus = surplus - addition
    return np.array([bound] + holding)


def ragged_sizes(own_key, amount, total, bound, lean):
    if amount == 2:
        one = jax.random.randint(own_key, (), max(1, total - bound), min(bound, total - 1) + 1)
        return jnp.stack([one, total - one])
    sizes = jnp.asarray(profile(amount, total, bound, lean), jnp.int32)
    pairs = (amount - 1) // 2
    giver, receiver = sizes[1:1 + 2 * pairs:2], sizes[2:2 + 2 * pairs:2]
    room = jnp.minimum(giver - 1, bound - receiver)
    passed = jax.random.randint(jax.random.fold_in(own_key, 1), (pairs,), 0, 1 << 20) % (room + 1)
    sizes = sizes.at[1:1 + 2 * pairs:2].set(giver - passed).at[2:2 + 2 * pairs:2].set(receiver + passed)
    return sizes[jax.random.permutation(jax.random.fold_in(own_key, 2), amount)]


def centred(key, dims, deviation, limit, split=(), kind=jnp.bfloat16):
    result = deviation * jax.random.normal(key, dims, jnp.float32)
    if split:
        result = result * shard_levels(key, dims, split, -0.22, 0.18)
    return jnp.clip(result, -limit, limit).astype(kind)


def setup_inputs(seed: int = 0, part: int = 0) -> dict:
    keys = jax.random.split(jax.random.key(seed), 8)
    own_keys = jax.random.split(jax.random.fold_in(keys[7], part), 8)
    layer_input = centred(own_keys[0], (QUERIES, LEN, D), 1.0, 6.0, ((1, 8), (2, 2)))
    out_grad = centred(own_keys[1], (QUERIES, LEN, D), 1.0, 6.0, ((1, 8), (2, 2)))
    proj_in = centred(keys[2], (KI, D), D ** -0.5, 0.0625, ((1, 2),))
    proj_out = centred(keys[3], (KO, D), D ** -0.5, 0.0625, ((1, 2),))
    counts = draw_counts(jax.random.fold_in(jax.random.fold_in(keys[7], part), 71), part)
    store_rows = centred(own_keys[5], (ROWS, KO * KI), 1.0, 6.0, ((0, 16),))
    doc_ids = jnp.searchsorted(jnp.cumsum(ragged_sizes(own_keys[6], DOCS, ROWS, MOST, 2)), jnp.arange(ROWS), side="right").astype(jnp.int32)
    return {"layer_input": layer_input, "out_grad": out_grad, "proj_in": proj_in, "proj_out": proj_out, "counts": counts, "store_rows": store_rows, "doc_ids": doc_ids}


def reference(layer_input, out_grad, proj_in, proj_out, counts, store_rows, doc_ids):
    in_factor = jnp.einsum("qtd,kd->qtk", layer_input.astype(jnp.float32), proj_in.astype(jnp.float32), precision=lax.Precision.HIGHEST)
    out_factor = jnp.einsum("qtd,kd->qtk", out_grad.astype(jnp.float32), proj_out.astype(jnp.float32), precision=lax.Precision.HIGHEST)
    positions = lax.broadcasted_iota(jnp.int32, (QUERIES, LEN), 1)
    token_weight = jnp.where(positions < counts[:, None], jnp.float32(1.0), jnp.float32(0.0)) / counts[:, None].astype(jnp.float32)
    weighted = out_factor * token_weight[:, :, None]
    query_grads = jnp.einsum("qto,qti->qoi", weighted, in_factor, precision=lax.Precision.HIGHEST).reshape(QUERIES, KO * KI)
    grads_low = query_grads.astype(jnp.bfloat16)
    row_scores = jnp.dot(grads_low, store_rows.T, preferred_element_type=jnp.float32)
    totals = jax.ops.segment_sum(row_scores.T, doc_ids, num_segments=DOCS)
    doc_scores = totals[doc_ids].T
    return query_grads, row_scores, doc_scores
```

```python
import functools
import math

import jax
import jax.numpy as jnp
from jax import lax
from jax.experimental import pallas as pl
from jax.experimental.pallas import tpu as pltpu
from jax.sharding import PartitionSpec as P

MESH = pl.DeviceIdType.MESH
NT = (((1,), (1,)), ((), ()))
TN = (((0,), (0,)), ((), ()))
EDGE = 64
F32, BF16 = jnp.float32, jnp.bfloat16


def split(value):
    high = value.astype(BF16)
    return high, (value - high.astype(F32)).astype(BF16)


def kernel(
    n, own,
    x_hbm, g_hbm, pi_hbm, po_hbm, cnt, rows_hbm, ids_ref,
    grads_out, rows_out, docs_out,
    x, g, pi, po, rows, fac, peer, gs, part, recv, full, edge_out, edge_in, ext, same,
    load_sem, mp_sem, edge_sem, rs_sem, ag_sem,
):
    queries, span, depth = x_hbm.shape
    half = queries // 2
    ki, ko = pi_hbm.shape[0], po_hbm.shape[0]
    width = ki * ko
    chunk = width // own
    step = n // own
    row_count = rows_hbm.shape[0]
    st, mp = lax.axis_index("store"), lax.axis_index("mp")
    me = st * 2 + mp

    def at(rank):
        return {"store": rank // 2, "mp": lax.rem(rank, 2)}

    def load(src, dst, k):
        copy = pltpu.make_async_copy(src, dst, load_sem.at[k])
        copy.start()
        return copy

    first, second = (1 - mp) * half, mp * half
    loads = [
        load(pi_hbm, pi, 0),
        load(x_hbm.at[pl.ds(first, half)], x.at[pl.ds(0, half)], 1),
        load(po_hbm, po, 2),
        load(g_hbm.at[pl.ds(first, half)], g.at[pl.ds(0, half)], 3),
        load(x_hbm.at[pl.ds(second, half)], x.at[pl.ds(half, half)], 4),
        load(g_hbm.at[pl.ds(second, half)], g.at[pl.ds(half, half)], 5),
        load(rows_hbm, rows, 6),
    ]

    barrier = pltpu.get_barrier_semaphore()

    @pl.loop(1, n)
    def _(k):
        pl.semaphore_signal(barrier, 1, device_id=at(lax.rem(me + k, n)), device_id_type=MESH)

    ids = ids_ref[...].astype(F32)
    across = jnp.broadcast_to(ids, (128, row_count)).T
    for b in range(row_count // 128):
        col = slice(b * 128, (b + 1) * 128)
        same[:, col] = jnp.where(across == ids[:, col], 1.0, 0.0).astype(BF16)

    def factors(h, kx, kg):
        loads[kx].wait()
        xi = x[h * half:(h + 1) * half].reshape(half * span, depth)
        fi = lax.dot_general(xi, pi[...], NT, preferred_element_type=F32)
        loads[kg].wait()
        gi = g[h * half:(h + 1) * half].reshape(half * span, depth)
        fo = lax.dot_general(gi, po[...], NT, preferred_element_type=F32)
        return fi, fo

    loads[0].wait()
    loads[2].wait()
    fi, fo = factors(0, 1, 3)
    fac[...] = jnp.concatenate([fi, fo], axis=1)
    pl.semaphore_wait(barrier, n - 1)
    to_peer = pltpu.make_async_remote_copy(
        src_ref=fac, dst_ref=peer, send_sem=mp_sem.at[0], recv_sem=mp_sem.at[1],
        device_id={"mp": 1 - mp}, device_id_type=MESH,
    )
    to_peer.start()
    fi, fo = factors(1, 4, 5)

    loads[6].wait()
    head_id, tail_id = ids[:, :1], ids[:, row_count - 1:]
    head_mask = jnp.where(ids[:, :EDGE] == head_id, 1.0, 0.0)
    tail_mask = jnp.where(ids[:, row_count - EDGE:] == tail_id, 1.0, 0.0)
    for e, (mask, lo, eid) in enumerate(
        ((head_mask, 0, head_id), (tail_mask, row_count - EDGE, tail_id))
    ):
        wide = jnp.broadcast_to(mask, (16, EDGE)).astype(BF16)
        total = jnp.dot(wide, rows[lo:lo + EDGE, :], preferred_element_type=F32)
        edge_out[e, :, :width] = total[:1]
        edge_out[e, :, width:] = jnp.broadcast_to(eid, (1, 128))
    edges = []
    for e, rank in enumerate((lax.rem(me + n - 1, n), lax.rem(me + 1, n))):
        copy = pltpu.make_async_remote_copy(
            src_ref=edge_out.at[e], dst_ref=edge_in.at[1 - e],
            send_sem=edge_sem.at[e], recv_sem=edge_sem.at[3 - e],
            device_id=at(rank), device_id_type=MESH,
        )
        copy.start()
        edges.append(copy)

    to_peer.wait_recv()
    fi = fi + peer[:, :ki]
    fo = fo + peer[:, ki:]
    pos = st * span + lax.broadcasted_iota(jnp.int32, (span, ko), 0)
    for k in range(half):
        count = cnt[second + k]
        weight = jnp.where(pos < count, 1.0, 0.0) / jnp.full((span, ko), count, jnp.int32).astype(F32)
        a_hi, a_lo = split(fo[k * span:(k + 1) * span] * weight)
        b_hi, b_lo = split(fi[k * span:(k + 1) * span])
        lhs = jnp.concatenate([a_hi, a_hi, a_lo], axis=0)
        rhs = jnp.concatenate([b_hi, b_lo, b_hi], axis=0)
        outer = lax.dot_general(lhs, jnp.concatenate([rhs, rhs], axis=1), TN, preferred_element_type=F32)
        gs[k * ko:(k + 1) * ko, :] = outer
    lower = lax.broadcasted_iota(jnp.int32, (half, 128), 1) < ki
    for j in range(width // 128):
        even = gs[pl.ds(2 * j, half, stride=ko), :]
        odd = gs[pl.ds(2 * j + 1, half, stride=ko), :]
        c, off = divmod(j * 128, chunk)
        part[c, :, off:off + 128] = jnp.where(lower, even, odd)

    mine = me // step
    is_owner = lax.rem(me, step) == 0

    def guarded(cond, fn):
        if own == n:
            fn()
        else:
            pl.when(cond)(fn)

    @pl.loop(1 if own == n else 0, own)
    def _(k):
        c = lax.rem(mine + k, own)
        rank = c * step

        def send():
            pltpu.make_async_remote_copy(
                src_ref=part.at[c], dst_ref=recv.at[me], send_sem=rs_sem.at[0],
                recv_sem=rs_sem.at[1], device_id=at(rank), device_id_type=MESH,
            ).start()

        guarded(rank != me, send)

    def drain(buf, count, sem):
        view = buf.at[pl.ds(0, count)]
        pltpu.make_async_copy(view, view, sem).wait()

    def combine():
        recv[me] = part[mine]
        drain(recv, n - 1, rs_sem.at[1])
        sums = []
        for m in range(2):
            total = recv[m]
            for s in range(1, n // 2):
                total = total + recv[2 * s + m]
            sums.append(total)
        full[mine] = jnp.concatenate(sums, axis=0)

        @pl.loop(1, n)
        def _(k):
            pltpu.make_async_remote_copy(
                src_ref=full.at[mine], dst_ref=full.at[mine], send_sem=ag_sem.at[0],
                recv_sem=ag_sem.at[1], device_id=at(lax.rem(me + k, n)), device_id_type=MESH,
            ).start()

    guarded(is_owner, combine)

    for copy in edges:
        copy.wait_recv()
    l_hi, l_lo = split(edge_in[0, :, :width])
    r_hi, r_lo = split(edge_in[1, :, :width])
    left_id = jnp.where(me == 0, -1.0, edge_in[0, :, width:width + 1])
    right_id = jnp.where(me == n - 1, -1.0, edge_in[1, :, width:width + 1])
    line = lax.broadcasted_iota(jnp.int32, (16, width), 0)
    stack = jnp.zeros((16, width), F32)
    for e, term in enumerate((l_hi, l_lo, r_hi, r_lo)):
        stack = jnp.where(line == e, term.astype(F32), stack)
    ext[...] = stack.astype(BF16)

    guarded(is_owner, lambda: drain(full, own - 1, ag_sem.at[1]))
    if own != n:
        pl.when(jnp.logical_not(is_owner))(lambda: drain(full, own, ag_sem.at[1]))

    grads = jnp.concatenate([full[c] for c in range(own)], axis=1)
    grads_out[...] = grads
    low = grads.astype(BF16)
    scores = lax.dot_general(low, rows[...], NT, preferred_element_type=F32)
    around = lax.dot_general(low, ext[...], NT, preferred_element_type=F32)
    rows_out[...] = scores
    s_hi, s_lo = split(scores)
    docs = jnp.dot(s_hi, same[...], preferred_element_type=F32) + jnp.dot(
        s_lo, same[...], preferred_element_type=F32
    )
    docs = docs + jnp.where(ids == left_id, around[:, 0:1] + around[:, 1:2], 0.0)
    docs = docs + jnp.where(ids == right_id, around[:, 2:3] + around[:, 3:4], 0.0)
    docs_out[...] = docs

    to_peer.wait_send()
    for copy in edges:
        copy.wait_send()
    if own == n:
        drain(part, own - 1, rs_sem.at[0])
        drain(full, n - 1, ag_sem.at[0])
    else:
        @pl.when(is_owner)
        def _():
            drain(part, own - 1, rs_sem.at[0])
            for _ in range((n - 1) // (own - 1)):
                drain(full, own - 1, ag_sem.at[0])
            if (n - 1) % (own - 1):
                drain(full, (n - 1) % (own - 1), ag_sem.at[0])

        @pl.when(jnp.logical_not(is_owner))
        def _():
            drain(part, own, rs_sem.at[0])


def local(layer_input, out_grad, proj_in, proj_out, counts, store_rows, doc_ids):
    n = lax.axis_size("store") * lax.axis_size("mp")
    queries, span, depth = layer_input.shape
    half = queries // 2
    ki, ko = proj_in.shape[0], proj_out.shape[0]
    width = ki * ko
    own = math.gcd(n, width // 128)
    chunk = width // own
    row_count = store_rows.shape[0]
    hbm = pl.BlockSpec(memory_space=pl.ANY)
    vmem = pl.BlockSpec(memory_space=pltpu.VMEM)
    smem = pl.BlockSpec(memory_space=pltpu.SMEM)
    return pl.pallas_call(
        functools.partial(kernel, n, own),
        out_shape=(
            jax.ShapeDtypeStruct((queries, width), F32),
            jax.ShapeDtypeStruct((queries, row_count), F32),
            jax.ShapeDtypeStruct((queries, row_count), F32),
        ),
        in_specs=[hbm, hbm, hbm, hbm, smem, hbm, vmem],
        out_specs=(vmem, vmem, vmem),
        scratch_shapes=[
            pltpu.VMEM(layer_input.shape, BF16),
            pltpu.VMEM(out_grad.shape, BF16),
            pltpu.VMEM(proj_in.shape, BF16),
            pltpu.VMEM(proj_out.shape, BF16),
            pltpu.VMEM(store_rows.shape, BF16),
            pltpu.VMEM((half * span, ki + ko), F32),
            pltpu.VMEM((half * span, ki + ko), F32),
            pltpu.VMEM((half * ko, 2 * ki), F32),
            pltpu.VMEM((own, half, chunk), F32),
            pltpu.VMEM((n, half, chunk), F32),
            pltpu.VMEM((own, queries, chunk), F32),
            pltpu.VMEM((2, 1, width + 128), F32),
            pltpu.VMEM((2, 1, width + 128), F32),
            pltpu.VMEM((16, width), BF16),
            pltpu.VMEM((row_count, row_count), BF16),
            pltpu.SemaphoreType.DMA((7,)),
            pltpu.SemaphoreType.DMA((2,)),
            pltpu.SemaphoreType.DMA((4,)),
            pltpu.SemaphoreType.DMA((2,)),
            pltpu.SemaphoreType.DMA((2,)),
        ],
        compiler_params=pltpu.CompilerParams(
            collective_id=0, has_side_effects=True, vmem_limit_bytes=62 * 1024 * 1024
        ),
    )(layer_input, out_grad, proj_in, proj_out, counts, store_rows, doc_ids.reshape(1, -1))


def solution(mesh):
    placed = (
        P("dom", "store", "mp"),
        P("dom", "store", "mp"),
        P(None, "mp"),
        P(None, "mp"),
        P("dom"),
        P(("dom", "store", "mp"), None),
        P(("dom", "store", "mp")),
    )
    return jax.shard_map(
        local,
        mesh=mesh,
        in_specs=placed,
        out_specs=(P("dom", None), P("dom", ("store", "mp")), P("dom", ("store", "mp"))),
        check_vma=False,
    )
```

```python
import functools
import math

import jax
import jax.numpy as jnp
from jax import lax
from jax.experimental import pallas as pl
from jax.experimental.pallas import tpu as pltpu
from jax.sharding import PartitionSpec as P

MESH = pl.DeviceIdType.MESH
NT = (((1,), (1,)), ((), ()))
TN = (((0,), (0,)), ((), ()))
EDGE = 64
F32, BF16 = jnp.float32, jnp.bfloat16


def split(value):
    high = value.astype(BF16)
    return high, (value - high.astype(F32)).astype(BF16)


def kernel(
    n, own,
    x_hbm, g_hbm, pi_hbm, po_hbm, cnt, rows_hbm, ids_ref,
    out,
    x, g, pi, po, rows, fac, peer, gs, part, recv, full, edge_out, edge_in, ext, same,
    load_sem, mp_sem, edge_sem, rs_sem, ag_sem,
):
    queries, span, depth = x_hbm.shape
    half = queries // 2
    ki, ko = pi_hbm.shape[0], po_hbm.shape[0]
    width = ki * ko
    chunk = width // own
    step = n // own
    row_count = rows_hbm.shape[0]
    st, mp = lax.axis_index("store"), lax.axis_index("mp")
    me = st * 2 + mp

    def at(rank):
        return {"store": rank // 2, "mp": lax.rem(rank, 2)}

    def load(src, dst, k):
        copy = pltpu.make_async_copy(src, dst, load_sem.at[k])
        copy.start()
        return copy

    first, second = (1 - mp) * half, mp * half
    loads = [
        load(pi_hbm, pi, 0),
        load(x_hbm.at[pl.ds(first, half)], x.at[pl.ds(0, half)], 1),
        load(po_hbm, po, 2),
        load(g_hbm.at[pl.ds(first, half)], g.at[pl.ds(0, half)], 3),
        load(x_hbm.at[pl.ds(second, half)], x.at[pl.ds(half, half)], 4),
        load(g_hbm.at[pl.ds(second, half)], g.at[pl.ds(half, half)], 5),
    ]

    barrier = pltpu.get_barrier_semaphore()

    @pl.loop(1, n)
    def _(k):
        pl.semaphore_signal(barrier, 1, device_id=at(lax.rem(me + k, n)), device_id_type=MESH)

    ids = ids_ref[...].astype(F32).reshape(1, row_count)
    across = jnp.broadcast_to(ids, (128, row_count)).T
    for b in range(row_count // 128):
        col = slice(b * 128, (b + 1) * 128)
        same[:, col] = jnp.where(across == ids[:, col], 1.0, 0.0).astype(BF16)

    def factors(h, kx, kg):
        loads[kx].wait()
        xi = x[h * half:(h + 1) * half].reshape(half * span, depth)
        fi = lax.dot_general(xi, pi[...], NT, preferred_element_type=F32)
        loads[kg].wait()
        gi = g[h * half:(h + 1) * half].reshape(half * span, depth)
        fo = lax.dot_general(gi, po[...], NT, preferred_element_type=F32)
        return fi, fo

    loads[0].wait()
    loads[2].wait()
    fi, fo = factors(0, 1, 3)
    fac[...] = jnp.concatenate([fi, fo], axis=1)
    pl.semaphore_wait(barrier, n - 1)
    to_peer = pltpu.make_async_remote_copy(
        src_ref=fac, dst_ref=peer, send_sem=mp_sem.at[0], recv_sem=mp_sem.at[1],
        device_id={"mp": 1 - mp}, device_id_type=MESH,
    )
    to_peer.start()
    loads.append(load(rows_hbm, rows, 6))
    fi, fo = factors(1, 4, 5)

    to_peer.wait_recv()
    fi = fi + peer[:, :ki]
    fo = fo + peer[:, ki:]
    pos = st * span + lax.broadcasted_iota(jnp.int32, (span, ko), 0)
    for k in range(half):
        count = cnt[second + k]
        weight = jnp.where(pos < count, 1.0, 0.0) / jnp.full((span, ko), count, jnp.int32).astype(F32)
        a_hi, a_lo = split(fo[k * span:(k + 1) * span] * weight)
        b_hi, b_lo = split(fi[k * span:(k + 1) * span])
        lhs = jnp.concatenate([a_hi, a_hi, a_lo], axis=0)
        rhs = jnp.concatenate([b_hi, b_lo, b_hi], axis=0)
        outer = lax.dot_general(lhs, jnp.concatenate([rhs, rhs], axis=1), TN, preferred_element_type=F32)
        gs[k * ko:(k + 1) * ko, :] = outer
    lower = lax.broadcasted_iota(jnp.int32, (half, 128), 1) < ki
    for j in range(width // 128):
        even = gs[pl.ds(2 * j, half, stride=ko), :]
        odd = gs[pl.ds(2 * j + 1, half, stride=ko), :]
        c, off = divmod(j * 128, chunk)
        part[c, :, off:off + 128] = jnp.where(lower, even, odd)

    mine = me // step
    is_owner = lax.rem(me, step) == 0

    def guarded(cond, fn):
        if own == n:
            fn()
        else:
            pl.when(cond)(fn)

    @pl.loop(1 if own == n else 0, own)
    def _(k):
        c = lax.rem(mine + k, own)
        rank = c * step

        def send():
            pltpu.make_async_remote_copy(
                src_ref=part.at[c], dst_ref=recv.at[me], send_sem=rs_sem.at[0],
                recv_sem=rs_sem.at[1], device_id=at(rank), device_id_type=MESH,
            ).start()

        guarded(rank != me, send)

    loads[6].wait()
    head_id, tail_id = ids[:, :1], ids[:, row_count - 1:]
    head_mask = jnp.where(ids[:, :EDGE] == head_id, 1.0, 0.0)
    tail_mask = jnp.where(ids[:, row_count - EDGE:] == tail_id, 1.0, 0.0)
    for e, (mask, lo, eid) in enumerate(
        ((head_mask, 0, head_id), (tail_mask, row_count - EDGE, tail_id))
    ):
        wide = jnp.broadcast_to(mask, (16, EDGE)).astype(BF16)
        total = jnp.dot(wide, rows[lo:lo + EDGE, :], preferred_element_type=F32)
        edge_out[e, :, :width] = total[:1]
        edge_out[e, :, width:] = jnp.broadcast_to(eid, (1, 128))
    edges = []
    for e, rank in enumerate((lax.rem(me + n - 1, n), lax.rem(me + 1, n))):
        copy = pltpu.make_async_remote_copy(
            src_ref=edge_out.at[e], dst_ref=edge_in.at[1 - e],
            send_sem=edge_sem.at[e], recv_sem=edge_sem.at[3 - e],
            device_id=at(rank), device_id_type=MESH,
        )
        copy.start()
        edges.append(copy)

    def drain(buf, count, sem):
        view = buf.at[pl.ds(0, count)]
        pltpu.make_async_copy(view, view, sem).wait()

    def combine():
        recv[me] = part[mine]
        drain(recv, n - 1, rs_sem.at[1])
        sums = []
        for m in range(2):
            total = recv[m]
            for s in range(1, n // 2):
                total = total + recv[2 * s + m]
            sums.append(total)
        full[mine] = jnp.concatenate(sums, axis=0)

        @pl.loop(1, n)
        def _(k):
            pltpu.make_async_remote_copy(
                src_ref=full.at[mine], dst_ref=full.at[mine], send_sem=ag_sem.at[0],
                recv_sem=ag_sem.at[1], device_id=at(lax.rem(me + k, n)), device_id_type=MESH,
            ).start()

    guarded(is_owner, combine)

    for copy in edges:
        copy.wait_recv()
    l_hi, l_lo = split(edge_in[0, :, :width])
    r_hi, r_lo = split(edge_in[1, :, :width])
    left_id = jnp.where(me == 0, -1.0, edge_in[0, :, width:width + 1])
    right_id = jnp.where(me == n - 1, -1.0, edge_in[1, :, width:width + 1])
    line = lax.broadcasted_iota(jnp.int32, (16, width), 0)
    stack = jnp.zeros((16, width), F32)
    for e, term in enumerate((l_hi, l_lo, r_hi, r_lo)):
        stack = jnp.where(line == e, term.astype(F32), stack)
    ext[...] = stack.astype(BF16)

    guarded(is_owner, lambda: drain(full, own - 1, ag_sem.at[1]))
    if own != n:
        pl.when(jnp.logical_not(is_owner))(lambda: drain(full, own, ag_sem.at[1]))

    grads = jnp.concatenate([full[c] for c in range(own)], axis=1)
    out[:, :width] = grads
    low = grads.astype(BF16)
    scores = lax.dot_general(low, rows[...], NT, preferred_element_type=F32)
    around = lax.dot_general(low, ext[...], NT, preferred_element_type=F32)
    out[:, width:width + row_count] = scores
    s_hi, s_lo = split(scores)
    docs = jnp.dot(s_hi, same[...], preferred_element_type=F32) + jnp.dot(
        s_lo, same[...], preferred_element_type=F32
    )
    docs = docs + jnp.where(ids == left_id, around[:, 0:1] + around[:, 1:2], 0.0)
    docs = docs + jnp.where(ids == right_id, around[:, 2:3] + around[:, 3:4], 0.0)
    out[:, width + row_count:] = docs

    to_peer.wait_send()
    for copy in edges:
        copy.wait_send()
    if own == n:
        drain(part, own - 1, rs_sem.at[0])
        drain(full, n - 1, ag_sem.at[0])
    else:
        @pl.when(is_owner)
        def _():
            drain(part, own - 1, rs_sem.at[0])
            for _ in range((n - 1) // (own - 1)):
                drain(full, own - 1, ag_sem.at[0])
            if (n - 1) % (own - 1):
                drain(full, (n - 1) % (own - 1), ag_sem.at[0])

        @pl.when(jnp.logical_not(is_owner))
        def _():
            drain(part, own, rs_sem.at[0])


def parts(joined, grads_out, rows_out, docs_out, sem):
    at = 0
    copies = []
    for k, out in enumerate((grads_out, rows_out, docs_out)):
        width = out.shape[1]
        copies.append(pltpu.make_async_copy(joined.at[:, at:at + width], out, sem.at[k]))
        copies[-1].start()
        at += width
    for copy in copies:
        copy.wait()


def hand_out(joined, width, row_count):
    queries = joined.shape[0]
    widths = (width, row_count, row_count)
    return pl.pallas_call(
        parts,
        out_shape=tuple(jax.ShapeDtypeStruct((queries, w), F32) for w in widths),
        in_specs=[pl.BlockSpec(memory_space=pltpu.VMEM)],
        out_specs=tuple(pl.BlockSpec(memory_space=pl.ANY) for _ in widths),
        scratch_shapes=[pltpu.SemaphoreType.DMA((3,))],
    )(joined)


def local(layer_input, out_grad, proj_in, proj_out, counts, store_rows, doc_ids):
    n = lax.axis_size("store") * lax.axis_size("mp")
    queries, span, depth = layer_input.shape
    half = queries // 2
    ki, ko = proj_in.shape[0], proj_out.shape[0]
    width = ki * ko
    own = math.gcd(n, width // 128)
    chunk = width // own
    row_count = store_rows.shape[0]
    hbm = pl.BlockSpec(memory_space=pl.ANY)
    vmem = pl.BlockSpec(memory_space=pltpu.VMEM)
    smem = pl.BlockSpec(memory_space=pltpu.SMEM)
    joined = pl.pallas_call(
        functools.partial(kernel, n, own),
        out_shape=jax.ShapeDtypeStruct((queries, width + 2 * row_count), F32),
        in_specs=[hbm, hbm, hbm, hbm, smem, hbm, vmem],
        out_specs=vmem,
        scratch_shapes=[
            pltpu.VMEM(layer_input.shape, BF16),
            pltpu.VMEM(out_grad.shape, BF16),
            pltpu.VMEM(proj_in.shape, BF16),
            pltpu.VMEM(proj_out.shape, BF16),
            pltpu.VMEM(store_rows.shape, BF16),
            pltpu.VMEM((half * span, ki + ko), F32),
            pltpu.VMEM((half * span, ki + ko), F32),
            pltpu.VMEM((half * ko, 2 * ki), F32),
            pltpu.VMEM((own, half, chunk), F32),
            pltpu.VMEM((n, half, chunk), F32),
            pltpu.VMEM((own, queries, chunk), F32),
            pltpu.VMEM((2, 1, width + 128), F32),
            pltpu.VMEM((2, 1, width + 128), F32),
            pltpu.VMEM((16, width), BF16),
            pltpu.VMEM((row_count, row_count), BF16),
            pltpu.SemaphoreType.DMA((7,)),
            pltpu.SemaphoreType.DMA((2,)),
            pltpu.SemaphoreType.DMA((4,)),
            pltpu.SemaphoreType.DMA((2,)),
            pltpu.SemaphoreType.DMA((2,)),
        ],
        compiler_params=pltpu.CompilerParams(
            collective_id=0, has_side_effects=True, vmem_limit_bytes=62 * 1024 * 1024
        ),
    )(layer_input, out_grad, proj_in, proj_out, counts, store_rows, doc_ids)
    return hand_out(joined, width, row_count)


def solution(mesh):
    placed = (
        P("dom", "store", "mp"),
        P("dom", "store", "mp"),
        P(None, "mp"),
        P(None, "mp"),
        P("dom"),
        P(("dom", "store", "mp"), None),
        P(("dom", "store", "mp")),
    )
    return jax.shard_map(
        local,
        mesh=mesh,
        in_specs=placed,
        out_specs=(P("dom", None), P("dom", ("store", "mp")), P("dom", ("store", "mp"))),
        check_vma=False,
    )
```

```python
import functools
import math

import jax
import jax.numpy as jnp
from jax import lax
from jax.experimental import pallas as pl
from jax.experimental.pallas import tpu as pltpu
from jax.sharding import PartitionSpec as P

MESH = pl.DeviceIdType.MESH
NT = (((1,), (1,)), ((), ()))
TN = (((0,), (0,)), ((), ()))
EDGE = 64
F32, BF16 = jnp.float32, jnp.bfloat16


def split(value):
    high = value.astype(BF16)
    return high, (value - high.astype(F32)).astype(BF16)


def kernel(
    n, own,
    x_hbm, g_hbm, pi_hbm, po_hbm, cnt, rows_hbm, ids_ref,
    out,
    x, g, pi, po, rows, fac, peer, gs, part, recv, full, edge_out, edge_in, ext, same,
    load_sem, mp_sem, edge_sem, rs_sem, ag_sem, slot_sem,
):
    queries, span, depth = x_hbm.shape
    half = queries // 2
    ki, ko = pi_hbm.shape[0], po_hbm.shape[0]
    width = ki * ko
    chunk = width // own
    step = n // own
    row_count = rows_hbm.shape[0]
    st, mp = lax.axis_index("store"), lax.axis_index("mp")
    me = st * 2 + mp

    def at(rank):
        return {"store": rank // 2, "mp": lax.rem(rank, 2)}

    def load(src, dst, k):
        copy = pltpu.make_async_copy(src, dst, load_sem.at[k])
        copy.start()
        return copy

    first, second = (1 - mp) * half, mp * half
    loads = {"pi": load(pi_hbm, pi, 0), "po": load(po_hbm, po, 1)}
    pair = half // 2
    for b in range(4):
        start = (first, second)[b // 2] + b % 2 * pair
        for k, (src, dst) in enumerate(((x_hbm, x), (g_hbm, g))):
            loads[b, k] = load(src.at[pl.ds(start, pair)], dst.at[pl.ds(b * pair, pair)], 2 + 2 * b + k)

    barrier = pltpu.get_barrier_semaphore()

    @pl.loop(1, n)
    def _(k):
        pl.semaphore_signal(barrier, 1, device_id=at(lax.rem(me + k, n)), device_id_type=MESH)

    ids = ids_ref[...].astype(F32).reshape(1, row_count)
    across = jnp.broadcast_to(ids, (128, row_count)).T
    for b in range(row_count // 128):
        col = slice(b * 128, (b + 1) * 128)
        same[:, col] = jnp.where(across == ids[:, col], 1.0, 0.0).astype(BF16)

    def factors(h):
        terms = [[], []]
        for b in (2 * h, 2 * h + 1):
            for k, (act, proj) in enumerate(((x, pi), (g, po))):
                loads[b, k].wait()
                block = act[b * pair:(b + 1) * pair].reshape(pair * span, depth)
                terms[k].append(lax.dot_general(block, proj[...], NT, preferred_element_type=F32))
        return [jnp.concatenate(t, axis=0) for t in terms]

    loads["pi"].wait()
    loads["po"].wait()
    fi, fo = factors(0)
    fac[...] = jnp.concatenate([fi, fo], axis=1)
    pl.semaphore_wait(barrier, n - 1)
    to_peer = pltpu.make_async_remote_copy(
        src_ref=fac, dst_ref=peer, send_sem=mp_sem.at[0], recv_sem=mp_sem.at[1],
        device_id={"mp": 1 - mp}, device_id_type=MESH,
    )
    to_peer.start()
    loads["rows"] = load(rows_hbm, rows, 10)
    fi, fo = factors(1)

    to_peer.wait_recv()
    fi = fi + peer[:, :ki]
    fo = fo + peer[:, ki:]
    pos = st * span + lax.broadcasted_iota(jnp.int32, (span, ko), 0)
    for k in range(half):
        count = cnt[second + k]
        weight = jnp.where(pos < count, 1.0, 0.0) / jnp.full((span, ko), count, jnp.int32).astype(F32)
        a_hi, a_lo = split(fo[k * span:(k + 1) * span] * weight)
        b_hi, b_lo = split(fi[k * span:(k + 1) * span])
        lhs = jnp.concatenate([a_hi, a_hi, a_lo], axis=0)
        rhs = jnp.concatenate([b_hi, b_lo, b_hi], axis=0)
        outer = lax.dot_general(lhs, jnp.concatenate([rhs, rhs], axis=1), TN, preferred_element_type=F32)
        gs[k * ko:(k + 1) * ko, :] = outer
    lower = lax.broadcasted_iota(jnp.int32, (half, 128), 1) < ki
    for j in range(width // 128):
        even = gs[pl.ds(2 * j, half, stride=ko), :]
        odd = gs[pl.ds(2 * j + 1, half, stride=ko), :]
        c, off = divmod(j * 128, chunk)
        part[c, :, off:off + 128] = jnp.where(lower, even, odd)

    mine = me // step
    is_owner = lax.rem(me, step) == 0

    def guarded(cond, fn):
        if own == n:
            fn()
        else:
            pl.when(cond)(fn)

    @pl.loop(1 if own == n else 0, own)
    def _(k):
        c = lax.rem(mine + k, own)
        rank = c * step

        def send():
            pltpu.make_async_remote_copy(
                src_ref=part.at[c], dst_ref=recv.at[me], send_sem=rs_sem.at[0],
                recv_sem=rs_sem.at[1], device_id=at(rank), device_id_type=MESH,
            ).start()

        guarded(rank != me, send)

    loads["rows"].wait()
    head_id, tail_id = ids[:, :1], ids[:, row_count - 1:]
    head_mask = jnp.where(ids[:, :EDGE] == head_id, 1.0, 0.0)
    tail_mask = jnp.where(ids[:, row_count - EDGE:] == tail_id, 1.0, 0.0)
    for e, (mask, lo, eid) in enumerate(
        ((head_mask, 0, head_id), (tail_mask, row_count - EDGE, tail_id))
    ):
        wide = jnp.broadcast_to(mask, (16, EDGE)).astype(BF16)
        total = jnp.dot(wide, rows[lo:lo + EDGE, :], preferred_element_type=F32)
        edge_out[e, :, :width] = total[:1]
        edge_out[e, :, width:] = jnp.broadcast_to(eid, (1, 128))
    edges = []
    for e, rank in enumerate((lax.rem(me + n - 1, n), lax.rem(me + 1, n))):
        copy = pltpu.make_async_remote_copy(
            src_ref=edge_out.at[e], dst_ref=edge_in.at[1 - e],
            send_sem=edge_sem.at[e], recv_sem=edge_sem.at[3 - e],
            device_id=at(rank), device_id_type=MESH,
        )
        copy.start()
        edges.append(copy)

    def drain(buf, count, sem):
        view = buf.at[pl.ds(0, count)]
        pltpu.make_async_copy(view, view, sem).wait()

    def combine():
        recv[me] = part[mine]
        drain(recv, n - 1, rs_sem.at[1])
        sums = []
        for m in range(2):
            total = recv[m]
            for s in range(1, n // 2):
                total = total + recv[2 * s + m]
            sums.append(total)
        full[mine] = jnp.concatenate(sums, axis=0)

        @pl.loop(1, n)
        def _(k):
            pltpu.make_async_remote_copy(
                src_ref=full.at[mine], dst_ref=full.at[mine], send_sem=ag_sem.at[0],
                recv_sem=slot_sem.at[me] if own == n else ag_sem.at[1], device_id=at(lax.rem(me + k, n)), device_id_type=MESH,
            ).start()

    guarded(is_owner, combine)

    for copy in edges:
        copy.wait_recv()
    l_hi, l_lo = split(edge_in[0, :, :width])
    r_hi, r_lo = split(edge_in[1, :, :width])
    left_id = jnp.where(me == 0, -1.0, edge_in[0, :, width:width + 1])
    right_id = jnp.where(me == n - 1, -1.0, edge_in[1, :, width:width + 1])
    line = lax.broadcasted_iota(jnp.int32, (16, width), 0)
    stack = jnp.zeros((16, width), F32)
    for e, term in enumerate((l_hi, l_lo, r_hi, r_lo)):
        stack = jnp.where(line == e, term.astype(F32), stack)
    ext[...] = stack.astype(BF16)

    if own == n:
        scores = jnp.zeros((queries, row_count), F32)
        around = jnp.zeros((queries, 16), F32)
        for k in range(n // 2):
            s = lax.rem(st - k + n // 2, n // 2)
            for m in range(2):
                c = 2 * s + m

                def land():
                    pltpu.make_async_copy(full.at[c], full.at[c], slot_sem.at[c]).wait()

                if k == 0:
                    pl.when(mp != m)(land)
                else:
                    land()
            grads = jnp.concatenate([full[2 * s], full[2 * s + 1]], axis=1)
            cols = pl.ds(pl.multiple_of(s * (2 * chunk), 2 * chunk), 2 * chunk)
            out[:, cols] = grads
            low = grads.astype(BF16)
            scores += lax.dot_general(low, rows[:, cols], NT, preferred_element_type=F32)
            around += lax.dot_general(low, ext[:, cols], NT, preferred_element_type=F32)
    else:
        pl.when(is_owner)(lambda: drain(full, own - 1, ag_sem.at[1]))
        pl.when(jnp.logical_not(is_owner))(lambda: drain(full, own, ag_sem.at[1]))
        grads = jnp.concatenate([full[c] for c in range(own)], axis=1)
        out[:, :width] = grads
        low = grads.astype(BF16)
        scores = lax.dot_general(low, rows[...], NT, preferred_element_type=F32)
        around = lax.dot_general(low, ext[...], NT, preferred_element_type=F32)
    out[:, width:width + row_count] = scores
    s_hi, s_lo = split(scores)
    docs = jnp.dot(s_hi, same[...], preferred_element_type=F32) + jnp.dot(
        s_lo, same[...], preferred_element_type=F32
    )
    docs = docs + jnp.where(ids == left_id, around[:, 0:1] + around[:, 1:2], 0.0)
    docs = docs + jnp.where(ids == right_id, around[:, 2:3] + around[:, 3:4], 0.0)
    out[:, width + row_count:] = docs

    to_peer.wait_send()
    for copy in edges:
        copy.wait_send()
    if own == n:
        drain(part, own - 1, rs_sem.at[0])
        drain(full, n - 1, ag_sem.at[0])
    else:
        @pl.when(is_owner)
        def _():
            drain(part, own - 1, rs_sem.at[0])
            for _ in range((n - 1) // (own - 1)):
                drain(full, own - 1, ag_sem.at[0])
            if (n - 1) % (own - 1):
                drain(full, (n - 1) % (own - 1), ag_sem.at[0])

        @pl.when(jnp.logical_not(is_owner))
        def _():
            drain(part, own, rs_sem.at[0])


def parts(joined, grads_out, rows_out, docs_out, sem):
    at = 0
    copies = []
    for k, out in enumerate((grads_out, rows_out, docs_out)):
        width = out.shape[1]
        copies.append(pltpu.make_async_copy(joined.at[:, at:at + width], out, sem.at[k]))
        copies[-1].start()
        at += width
    for copy in copies:
        copy.wait()


def hand_out(joined, width, row_count):
    queries = joined.shape[0]
    widths = (width, row_count, row_count)
    return pl.pallas_call(
        parts,
        out_shape=tuple(jax.ShapeDtypeStruct((queries, w), F32) for w in widths),
        in_specs=[pl.BlockSpec(memory_space=pltpu.VMEM)],
        out_specs=tuple(pl.BlockSpec(memory_space=pl.ANY) for _ in widths),
        scratch_shapes=[pltpu.SemaphoreType.DMA((3,))],
    )(joined)


def local(layer_input, out_grad, proj_in, proj_out, counts, store_rows, doc_ids):
    n = lax.axis_size("store") * lax.axis_size("mp")
    queries, span, depth = layer_input.shape
    half = queries // 2
    ki, ko = proj_in.shape[0], proj_out.shape[0]
    width = ki * ko
    own = math.gcd(n, width // 128)
    chunk = width // own
    row_count = store_rows.shape[0]
    hbm = pl.BlockSpec(memory_space=pl.ANY)
    vmem = pl.BlockSpec(memory_space=pltpu.VMEM)
    smem = pl.BlockSpec(memory_space=pltpu.SMEM)
    joined = pl.pallas_call(
        functools.partial(kernel, n, own),
        out_shape=jax.ShapeDtypeStruct((queries, width + 2 * row_count), F32),
        in_specs=[hbm, hbm, hbm, hbm, smem, hbm, vmem],
        out_specs=vmem,
        scratch_shapes=[
            pltpu.VMEM(layer_input.shape, BF16),
            pltpu.VMEM(out_grad.shape, BF16),
            pltpu.VMEM(proj_in.shape, BF16),
            pltpu.VMEM(proj_out.shape, BF16),
            pltpu.VMEM(store_rows.shape, BF16),
            pltpu.VMEM((half * span, ki + ko), F32),
            pltpu.VMEM((half * span, ki + ko), F32),
            pltpu.VMEM((half * ko, 2 * ki), F32),
            pltpu.VMEM((own, half, chunk), F32),
            pltpu.VMEM((n, half, chunk), F32),
            pltpu.VMEM((own, queries, chunk), F32),
            pltpu.VMEM((2, 1, width + 128), F32),
            pltpu.VMEM((2, 1, width + 128), F32),
            pltpu.VMEM((16, width), BF16),
            pltpu.VMEM((row_count, row_count), BF16),
            pltpu.SemaphoreType.DMA((11,)),
            pltpu.SemaphoreType.DMA((2,)),
            pltpu.SemaphoreType.DMA((4,)),
            pltpu.SemaphoreType.DMA((2,)),
            pltpu.SemaphoreType.DMA((2,)),
            pltpu.SemaphoreType.DMA((n,)),
        ],
        compiler_params=pltpu.CompilerParams(
            collective_id=0, has_side_effects=True, vmem_limit_bytes=62 * 1024 * 1024
        ),
    )(layer_input, out_grad, proj_in, proj_out, counts, store_rows, doc_ids)
    return hand_out(joined, width, row_count)


def solution(mesh):
    placed = (
        P("dom", "store", "mp"),
        P("dom", "store", "mp"),
        P(None, "mp"),
        P(None, "mp"),
        P("dom"),
        P(("dom", "store", "mp"), None),
        P(("dom", "store", "mp")),
    )
    return jax.shard_map(
        local,
        mesh=mesh,
        in_specs=placed,
        out_specs=(P("dom", None), P("dom", ("store", "mp")), P("dom", ("store", "mp"))),
        check_vma=False,
    )
```
